32 devices in a mesh: groups: 2 (over y), feat: 4 (over z), dp: 4 (over x, core).
Axes of the slice: x: 2, y: 2, z: 4, core: 2. Of those that a mesh axis runs over, the one named last changes fastest.
Arguments:
- features: bfloat16 [2048, 8192], P(('groups', 'dp'), 'feat'), parts along dimension 0, may hold values from -6 to 6
- bn_gain: float32 [8192], P('feat'), may hold values from 0.1 to 1.9
- bn_shift: float32 [8192], P('feat'), may hold values from -0.5 to 0.5
- weight: bfloat16 [8192, 8192], P('feat'), may hold values from -2 to 2
Outputs:
- covariance: float32 [16384, 8192], P(('groups', 'dp'), 'feat'), parts along dimension 0
- grad_in: bfloat16 [2048, 8192], P(('groups', 'dp'), 'feat'), parts along dimension 0
The draws below stay inside these ranges and needn't reach their ends.
There are 2 independent parts, one for each index of `groups`. The reference program is written for one: setup_inputs(seed, part) draws one part's arguments, and reference() takes and returns one part's arrays. A program takes and returns all parts, laid end to end along the dimension named above; an argument that names none is the same for every part. Nothing has to cross between parts.
All inputs are finite; a program needn't handle non-finite values.
Results may differ from the reference program's by a relative error of at most 0.014.
Values may be sent and summed in bfloat16 or wider, within the bound.
A program may use at most 256 MiB of HBM per device.

```python
import math
import jax
import jax.numpy as jnp
from jax import lax

D = 8192
D2 = 8192
IMAGES = 1024


def draw_weight(key, part):
    first, second = jax.random.split(key)
    base = jnp.clip(jax.random.normal(first, (D, D2), jnp.float32), -4.0, 4.0)
    column = jnp.exp(jax.random.uniform(second, (1, D2), jnp.float32, math.log(0.3), math.log(3.0)))
    return (base * column / math.sqrt(D)).astype(jnp.bfloat16)


def level_of(rng, shape, cuts, low, high):
    def one(position, blocks):
        heights = jax.random.uniform(jax.random.fold_in(jax.random.fold_in(rng, 6), position), (blocks,), jnp.float32, low / len(cuts), high / len(cuts))
        return jnp.repeat(jnp.exp(heights), shape[position] // blocks).reshape((-1,) + (1,) * (len(shape) - position - 1))

    gain = one(*cuts[0])
    for cut in cuts[1:]:
        gain = gain * one(*cut)
    return gain


def normal_values(stream_key, dims, deviation, reach, cuts=(), kind=jnp.bfloat16):
    array = deviation * jax.random.normal(stream_key, dims, jnp.float32)
    if cuts:
        array = array * level_of(stream_key, dims, cuts, -0.22, 0.18)
    return jnp.clip(array, -reach, reach).astype(kind)


def setup_inputs(seed: int = 0, part: int = 0) -> dict:
    seeds = jax.random.split(jax.random.key(seed), 5)
    own_keys = jax.random.split(jax.random.fold_in(seeds[4], part), 5)
    return {
        "features": normal_values(own_keys[0], (IMAGES, D), 1.0, 6.0, ((0, 4), (1, 4))),
        "bn_gain": jnp.clip(1.0 + 0.18 * jax.random.normal(seeds[1], (D,), jnp.float32), 0.1, 1.9),
        "bn_shift": jnp.clip(jax.random.uniform(seeds[2], (D,), jnp.float32, -0.5, 0.5) * level_of(seeds[2], (D,), ((0, 4),), -0.4, 0.0), -0.5, 0.5),
        "weight": draw_weight(jax.random.fold_in(seeds[4], 71), part),
    }


def reference(features, bn_gain, bn_shift, weight):
    rows = IMAGES
    hidden = features.astype(jnp.float32)
    mean_h = lax.optimization_barrier(jnp.sum(hidden, 0)) / rows
    var_h = lax.optimization_barrier(jnp.sum(hidden * hidden, 0)) / rows - mean_h * mean_h
    normed = (hidden - mean_h) * lax.rsqrt(var_h + 1e-05) * bn_gain + bn_shift
    activated = jnp.maximum(normed, 0.0).astype(jnp.bfloat16)
    projected = jnp.dot(activated, weight, preferred_element_type=jnp.float32).astype(jnp.bfloat16)
    proj_f = projected.astype(jnp.float32)
    proj_mean = lax.optimization_barrier(jnp.sum(proj_f, 0)) / rows
    centered = (proj_f - proj_mean).astype(jnp.bfloat16)
    cent_f = centered.astype(jnp.float32)
    proj_var = lax.optimization_barrier(jnp.sum(cent_f * cent_f, 0)) / (rows - 1)
    spread = jnp.sqrt(proj_var + 0.0001)
    covariance = jnp.dot(centered.T, centered, preferred_element_type=jnp.float32) / (rows - 1)
    row_ids = jnp.arange(D2)[:, None]
    col_ids = jnp.arange(D2)[None, :]
    off_diag = jnp.where(row_ids == col_ids, 0.0, covariance).astype(jnp.bfloat16)
    mixed = jnp.dot(centered, off_diag, preferred_element_type=jnp.float32)
    scale_up = rows / (rows - 1)
    active = jnp.where(spread < 1.0, 1.0 / spread, 0.0)
    grad_proj = (4.0 * scale_up * mixed - 25.0 * scale_up * active * cent_f).astype(jnp.bfloat16)
    grad_in = jnp.dot(grad_proj, weight.T, preferred_element_type=jnp.float32).astype(jnp.bfloat16)
    return (covariance, grad_in)
```

```python
import jax
import jax.numpy as jnp
from jax import lax
from jax.sharding import PartitionSpec as P


def shards(features, bn_gain, bn_shift, weight):
    dp_count = lax.axis_size("dp")
    feat_count = lax.axis_size("feat")
    local_rows = features.shape[0]
    images = local_rows * dp_count
    hidden = features.astype(jnp.float32)
    col_sums, col_squares = lax.psum((jnp.sum(hidden, 0), jnp.sum(hidden * hidden, 0)), "dp")
    mean_h = col_sums / images
    var_h = col_squares / images - mean_h * mean_h
    normed = (hidden - mean_h) * lax.rsqrt(var_h + 1e-05) * bn_gain + bn_shift
    activated = jnp.maximum(normed, 0.0).astype(jnp.bfloat16)
    partial_value = jnp.dot(activated, weight, preferred_element_type=jnp.float32).astype(jnp.bfloat16)
    proj_f = lax.psum_scatter(partial_value, "feat", scatter_dimension=1, tiled=True).astype(jnp.float32)
    proj_mean = lax.psum(jnp.sum(proj_f, 0), "dp") / images
    centered = (proj_f - proj_mean).astype(jnp.bfloat16)
    cent_full = lax.all_gather(centered, "feat", axis=1, tiled=True)
    piece = lax.all_gather(centered, "dp", axis=0, tiled=True)
    cent_x = lax.all_to_all(cent_full, "dp", split_axis=1, concat_axis=0, tiled=True)

    gram = lax.psum(
        lax.dot_general(centered, piece, (((1,), (1,)), ((), ())), preferred_element_type=jnp.float32),
        "feat",
    )
    piece_f = piece.astype(jnp.float32)
    proj_var = jnp.sum(piece_f * piece_f, 0) / (images - 1)
    spread = jnp.sqrt(proj_var + 0.0001)
    scale_up = images / (images - 1)
    active = jnp.where(spread < 1.0, 1.0 / spread, 0.0)
    factor = lax.all_gather(
        4.0 * scale_up * proj_var + 25.0 * scale_up * active, "feat", axis=0, tiled=True
    )
    scaled = (cent_full.astype(jnp.float32) * factor).astype(jnp.bfloat16)
    dims = (((1,), (1,)), ((), ()))
    through = lax.dot_general(cent_full, weight, dims, preferred_element_type=jnp.float32)
    direct = lax.dot_general(scaled, weight, dims, preferred_element_type=jnp.float32)
    through_all = lax.all_gather(through.astype(jnp.bfloat16), "dp", axis=0, tiled=True)

    covariance = lax.dot_general(
        cent_x, piece, (((0,), (0,)), ((), ())), preferred_element_type=jnp.float32
    ) / (images - 1)

    own = lax.axis_index("dp") * local_rows + jnp.arange(local_rows, dtype=jnp.int32)[:, None]
    same = own == jnp.arange(images, dtype=jnp.int32)[None, :]
    gram = gram * (4.0 * scale_up / (images - 1))
    diag = jnp.sum(jnp.where(same, gram, 0.0), 1, keepdims=True)
    rest = jnp.where(same, 0.0, gram).astype(jnp.bfloat16)
    grad_in = (
        jnp.dot(rest, through_all, preferred_element_type=jnp.float32) + diag * through - direct
    )
    return (covariance, grad_in.astype(jnp.bfloat16))


def solution(mesh):
    in_specs = (P(("groups", "dp"), "feat"), P("feat"), P("feat"), P("feat", None))
    out_specs = (P(("groups", "dp"), "feat"), P(("groups", "dp"), "feat"))
    return jax.shard_map(shards, mesh=mesh, in_specs=in_specs, out_specs=out_specs, check_vma=False)
```

```python
import jax
import jax.numpy as jnp
from jax import lax
from jax.sharding import PartitionSpec as P


def swap(value, distance):
    count = lax.axis_size("dp")
    return lax.ppermute(value, "dp", [(i, i ^ distance) for i in range(count)])


def block_order(count):
    order = [0]
    bit = count // 2
    while bit:
        order = order + [o ^ bit for o in order]
        bit //= 2
    return order


def gather_rows(value):
    bit = lax.axis_size("dp") // 2
    while bit:
        value = jnp.concatenate([value, swap(value, bit)], 0)
        bit //= 2
    return value


def column_blocks(full):
    count = lax.axis_size("dp")
    width = full.shape[1] // count
    me = lax.axis_index("dp")
    return [
        lax.dynamic_slice_in_dim(full, (me ^ o) * width, width, 1) for o in block_order(count)
    ]


def exchange(blocks):
    order = block_order(lax.axis_size("dp"))
    return jnp.concatenate([swap(b, o) if o else b for b, o in zip(blocks, order)], 0)


def shards(features, bn_gain, bn_shift, weight):
    dp_count = lax.axis_size("dp")
    feat_count = lax.axis_size("feat")
    local_rows = features.shape[0]
    images = local_rows * dp_count
    hidden = features.astype(jnp.float32)
    col_sums, col_squares = lax.psum((jnp.sum(hidden, 0), jnp.sum(hidden * hidden, 0)), "dp")
    mean_h = col_sums / images
    var_h = col_squares / images - mean_h * mean_h
    normed = (hidden - mean_h) * lax.rsqrt(var_h + 1e-05) * bn_gain + bn_shift
    activated = jnp.maximum(normed, 0.0).astype(jnp.bfloat16)
    partial_value = jnp.dot(activated, weight, preferred_element_type=jnp.float32).astype(jnp.bfloat16)
    proj_f = lax.psum_scatter(partial_value, "feat", scatter_dimension=1, tiled=True).astype(jnp.float32)
    proj_mean = lax.psum(jnp.sum(proj_f, 0), "dp") / images
    centered = (proj_f - proj_mean).astype(jnp.bfloat16)
    cent_full = lax.all_gather(centered, "feat", axis=1, tiled=True)
    piece = gather_rows(centered)

    gram = lax.dot_general(
        centered, piece, (((1,), (1,)), ((), ())), preferred_element_type=jnp.float32
    )
    piece_f = piece.astype(jnp.float32)
    proj_var = jnp.sum(piece_f * piece_f, 0) / (images - 1)
    spread = jnp.sqrt(proj_var + 0.0001)
    scale_up = images / (images - 1)
    active = jnp.where(spread < 1.0, 1.0 / spread, 0.0)
    factor = lax.all_gather(
        4.0 * scale_up * proj_var + 25.0 * scale_up * active, "feat", axis=0, tiled=True
    )
    cent_full, factor, _ = lax.optimization_barrier((cent_full, factor, gram))
    gram = lax.psum(gram, "feat")
    cent_full, cuts = lax.optimization_barrier((cent_full, column_blocks(cent_full)))
    cent_x = exchange(cuts)
    scaled = (cent_full.astype(jnp.float32) * factor).astype(jnp.bfloat16)
    dims = (((1,), (1,)), ((), ()))
    through = lax.dot_general(cent_full, weight, dims, preferred_element_type=jnp.float32)
    direct = lax.dot_general(scaled, weight, dims, preferred_element_type=jnp.float32)
    through_all = gather_rows(through.astype(jnp.bfloat16))

    covariance = lax.dot_general(
        cent_x, piece, (((0,), (0,)), ((), ())), preferred_element_type=jnp.float32
    ) / (images - 1)

    gram, covariance = lax.optimization_barrier((gram, covariance))
    own = jnp.arange(local_rows, dtype=jnp.int32)[:, None]
    same = own == jnp.arange(images, dtype=jnp.int32)[None, :]
    gram = gram * (4.0 * scale_up / (images - 1))
    diag = jnp.sum(jnp.where(same, gram, 0.0), 1, keepdims=True)
    rest = jnp.where(same, 0.0, gram).astype(jnp.bfloat16)
    grad_in = (
        jnp.dot(rest, through_all, preferred_element_type=jnp.float32) + diag * through - direct
    )
    return (covariance, grad_in.astype(jnp.bfloat16))


def solution(mesh):
    in_specs = (P(("groups", "dp"), "feat"), P("feat"), P("feat"), P("feat", None))
    out_specs = (P(("groups", "dp"), "feat"), P(("groups", "dp"), "feat"))
    return jax.shard_map(shards, mesh=mesh, in_specs=in_specs, out_specs=out_specs, check_vma=False)
```

```python
import jax
import jax.numpy as jnp
from jax import lax
from jax.sharding import PartitionSpec as P


def swap(value, distance):
    count = lax.axis_size("dp")
    return lax.ppermute(value, "dp", [(i, i ^ distance) for i in range(count)])


def block_order(count):
    order = [0]
    bit = count // 2
    while bit:
        order = order + [o ^ bit for o in order]
        bit //= 2
    return order


def gather_rows(value):
    bit = lax.axis_size("dp") // 2
    while bit:
        value = jnp.concatenate([value, swap(value, bit)], 0)
        bit //= 2
    return value


def column_blocks(full):
    count = lax.axis_size("dp")
    width = full.shape[1] // count
    me = lax.axis_index("dp")
    return [
        lax.dynamic_slice_in_dim(full, (me ^ o) * width, width, 1) for o in block_order(count)
    ]


def exchange(blocks):
    order = block_order(lax.axis_size("dp"))
    return [swap(b, o) if o else b for b, o in zip(blocks, order)]


def shards(features, bn_gain, bn_shift, weight):
    dp_count = lax.axis_size("dp")
    feat_count = lax.axis_size("feat")
    local_rows = features.shape[0]
    images = local_rows * dp_count
    hidden = features.astype(jnp.float32)
    col_sums, col_squares = lax.psum((jnp.sum(hidden, 0), jnp.sum(hidden * hidden, 0)), "dp")
    mean_h = col_sums / images
    var_h = col_squares / images - mean_h * mean_h
    normed = (hidden - mean_h) * lax.rsqrt(var_h + 1e-05) * bn_gain + bn_shift
    activated = jnp.maximum(normed, 0.0).astype(jnp.bfloat16)
    partial_value = jnp.dot(activated, weight, preferred_element_type=jnp.float32).astype(jnp.bfloat16)
    proj_f = lax.psum_scatter(partial_value, "feat", scatter_dimension=1, tiled=True).astype(jnp.float32)
    proj_mean = lax.psum(jnp.sum(proj_f, 0), "dp") / images
    centered = (proj_f - proj_mean).astype(jnp.bfloat16)
    half = local_rows // 2
    upper = lax.all_gather(centered[:half], "feat", axis=1, tiled=True)
    lower = lax.all_gather(centered[half:], "feat", axis=1, tiled=True)
    piece = gather_rows(centered)

    gram = lax.dot_general(
        centered, piece, (((1,), (1,)), ((), ())), preferred_element_type=jnp.float32
    )
    piece_f = piece.astype(jnp.float32)
    proj_var = jnp.sum(piece_f * piece_f, 0) / (images - 1)
    spread = jnp.sqrt(proj_var + 0.0001)
    scale_up = images / (images - 1)
    active = jnp.where(spread < 1.0, 1.0 / spread, 0.0)
    factor = lax.all_gather(
        4.0 * scale_up * proj_var + 25.0 * scale_up * active, "feat", axis=0, tiled=True
    )
    upper_cuts = exchange(column_blocks(upper))
    lower, factor, _ = lax.optimization_barrier((lower, factor, gram))
    gram = lax.psum(gram, "feat")
    lower, cuts = lax.optimization_barrier((lower, column_blocks(lower)))
    lower_cuts = exchange(cuts)
    cent_x = jnp.concatenate([b for pair in zip(upper_cuts, lower_cuts) for b in pair], 0)
    cent_full = jnp.concatenate([upper, lower], 0)
    dims = (((1,), (1,)), ((), ()))
    through = lax.dot_general(cent_full, weight, dims, preferred_element_type=jnp.float32)
    cent_full, through = lax.optimization_barrier((cent_full, through))
    scaled = (cent_full.astype(jnp.float32) * factor).astype(jnp.bfloat16)
    direct = lax.dot_general(scaled, weight, dims, preferred_element_type=jnp.float32)
    through_all = gather_rows(through.astype(jnp.bfloat16))

    covariance = lax.dot_general(
        cent_x, piece, (((0,), (0,)), ((), ())), preferred_element_type=jnp.float32
    ) / (images - 1)

    gram, covariance = lax.optimization_barrier((gram, covariance))
    own = jnp.arange(local_rows, dtype=jnp.int32)[:, None]
    same = own == jnp.arange(images, dtype=jnp.int32)[None, :]
    gram = gram * (4.0 * scale_up / (images - 1))
    diag = jnp.sum(jnp.where(same, gram, 0.0), 1, keepdims=True)
    rest = jnp.where(same, 0.0, gram).astype(jnp.bfloat16)
    grad_in = (
        jnp.dot(rest, through_all, preferred_element_type=jnp.float32) + diag * through - direct
    )
    return (covariance, grad_in.astype(jnp.bfloat16))


def solution(mesh):
    in_specs = (P(("groups", "dp"), "feat"), P("feat"), P("feat"), P("feat", None))
    out_specs = (P(("groups", "dp"), "feat"), P(("groups", "dp"), "feat"))
    return jax.shard_map(shards, mesh=mesh, in_specs=in_specs, out_specs=out_specs, check_vma=False)
```

```python
import jax
import jax.numpy as jnp
from jax import lax
from jax.sharding import PartitionSpec as P


def swap(value, distance):
    count = lax.axis_size("dp")
    return lax.ppermute(value, "dp", [(i, i ^ distance) for i in range(count)])


def block_order(count):
    order = [0]
    bit = count // 2
    while bit:
        order = order + [o ^ bit for o in order]
        bit //= 2
    return order


def gather_rows(value):
    bit = lax.axis_size("dp") // 2
    while bit:
        value = jnp.concatenate([value, swap(value, bit)], 0)
        bit //= 2
    return value


def column_blocks(full):
    count = lax.axis_size("dp")
    width = full.shape[1] // count
    me = lax.axis_index("dp")
    return [
        lax.dynamic_slice_in_dim(full, (me ^ o) * width, width, 1) for o in block_order(count)
    ]


def exchange(blocks):
    order = block_order(lax.axis_size("dp"))
    return [swap(b, o) if o else b for b, o in zip(blocks, order)]


def shards(features, bn_gain, bn_shift, weight):
    dp_count = lax.axis_size("dp")
    feat_count = lax.axis_size("feat")
    local_rows = features.shape[0]
    images = local_rows * dp_count
    hidden = features.astype(jnp.float32)
    col_sums, col_squares = lax.psum((jnp.sum(hidden, 0), jnp.sum(hidden * hidden, 0)), "dp")
    mean_h = col_sums / images
    var_h = col_squares / images - mean_h * mean_h
    normed = (hidden - mean_h) * lax.rsqrt(var_h + 1e-05) * bn_gain + bn_shift
    activated = jnp.maximum(normed, 0.0).astype(jnp.bfloat16)
    partial_value = jnp.dot(activated, weight, preferred_element_type=jnp.float32).astype(jnp.bfloat16)
    proj_f = lax.psum_scatter(partial_value, "feat", scatter_dimension=1, tiled=True).astype(jnp.float32)
    proj_mean = lax.psum(jnp.sum(proj_f, 0), "dp") / images
    centered = (proj_f - proj_mean).astype(jnp.bfloat16)
    cent_full = lax.all_gather(centered, "feat", axis=1, tiled=True)
    piece = gather_rows(centered)

    gram = lax.dot_general(
        centered, piece, (((1,), (1,)), ((), ())), preferred_element_type=jnp.float32
    )
    piece_f = piece.astype(jnp.float32)
    proj_var = jnp.sum(piece_f * piece_f, 0) / (images - 1)
    spread = jnp.sqrt(proj_var + 0.0001)
    scale_up = images / (images - 1)
    active = jnp.where(spread < 1.0, 1.0 / spread, 0.0)
    factor = lax.all_gather(
        4.0 * scale_up * proj_var + 25.0 * scale_up * active, "feat", axis=0, tiled=True
    )
    cent_full, factor, _ = lax.optimization_barrier((cent_full, factor, gram))
    gram = lax.psum(gram, "feat")
    cent_full, cuts = lax.optimization_barrier((cent_full, column_blocks(cent_full)))
    blocks = exchange(cuts)
    scaled = (cent_full.astype(jnp.float32) * factor).astype(jnp.bfloat16)
    dims = (((1,), (1,)), ((), ()))
    direct = lax.dot_general(scaled, weight, dims, preferred_element_type=jnp.float32)
    cent_full, direct, gram, blocks = lax.optimization_barrier((cent_full, direct, gram, blocks))
    cent_x = jnp.concatenate(blocks, 0)
    through = lax.dot_general(cent_full, weight, dims, preferred_element_type=jnp.float32)
    through_all = gather_rows(through.astype(jnp.bfloat16))

    covariance = lax.dot_general(
        cent_x, piece, (((0,), (0,)), ((), ())), preferred_element_type=jnp.float32
    ) / (images - 1)

    gram, covariance = lax.optimization_barrier((gram, covariance))
    own = jnp.arange(local_rows, dtype=jnp.int32)[:, None]
    same = own == jnp.arange(images, dtype=jnp.int32)[None, :]
    gram = gram * (4.0 * scale_up / (images - 1))
    diag = jnp.sum(jnp.where(same, gram, 0.0), 1, keepdims=True)
    rest = jnp.where(same, 0.0, gram).astype(jnp.bfloat16)
    grad_in = (
        jnp.dot(rest, through_all, preferred_element_type=jnp.float32) + diag * through - direct
    )
    return (covariance, grad_in.astype(jnp.bfloat16))


def solution(mesh):
    in_specs = (P(("groups", "dp"), "feat"), P("feat"), P("feat"), P("feat", None))
    out_specs = (P(("groups", "dp"), "feat"), P(("groups", "dp"), "feat"))
    return jax.shard_map(shards, mesh=mesh, in_specs=in_specs, out_specs=out_specs, check_vma=False)
```
